32 devices in a mesh: feed: 4 (over y, core), chan: 8 (over z, x).
Axes of the slice: x: 2, y: 2, z: 4, core: 2. Of those that a mesh axis runs over, the one named last changes fastest.
Arguments:
- voltages: bfloat16 [2, 2, 8, 4096, 1024], P(None, None, 'chan', None, 'feed'), may hold values from -6 to 6
- history: bfloat16 [2, 2, 8, 48, 1024], P(None, None, 'chan', None, 'feed'), may hold values from -6 to 6
- gains: float32 [2, 2, 8, 1024], P(None, None, 'chan', 'feed'), may hold values from -4 to 4
- weights: bfloat16 [2, 8, 1024, 1024], P(None, 'chan'), may hold values from -0.09375 to 0.09375
- beam_lists: int32 [8, 256], replicated, may hold values from 0 to 1023, as said below
- beam_counts: int32 [8], replicated, may hold values from 1 to 256, as said below
Outputs:
- power_blocks: bfloat16 [128, 128, 2048], P('feed', None, 'chan')
The draws below stay inside these ranges and needn't reach their ends.
Inputs may be any that keep to these rules, and one draw needn't show every extreme that they name: `beam_lists`: row n holds in its first beam_counts[n] entries, in increasing order, the beams that node n owns, and 0 in the others; every beam is owned by exactly one node. `beam_counts`: the counts sum to 1024; some node owns exactly 256 beams.
All inputs are finite; a program needn't handle non-finite values.
Results may differ from the reference program's by a relative error of at most 0.013.
Values may be sent and summed in bfloat16 or wider, within the bound.
A program may use at most 192 MiB of HBM per device.

```python
import math
import jax
import jax.numpy as jnp
from jax import lax

FEEDS = 1024
BEAMS = 1024
POLS = 2
U = 16
TAPS = 4
TINT = 2
NODES = 8
COARSE = 8
CHANS = 128
SPECTRA = 256
SAMPLES = 4096
HIST = 48
BINS = 128
MOST = 256


def owner_plan(key):
    base_key = jax.random.fold_in(key, 7)
    key_busy, key_swing, key_shuffle, key_beams = jax.random.split(base_key, 4)
    others = NODES - 1
    base_load = (BEAMS - MOST) // others
    remainder = (BEAMS - MOST) % others
    pair_count = others // 2
    busiest = jax.random.randint(key_busy, (), 0, NODES, dtype=jnp.int32)
    swing = jax.random.randint(key_swing, (pair_count,), -(base_load // 2), base_load // 2 + 1, dtype=jnp.int32)
    shifts = jnp.zeros((others,), jnp.int32)
    pair_ids = jnp.arange(pair_count, dtype=jnp.int32) * 2
    shifts = shifts.at[pair_ids].set(swing).at[pair_ids + 1].set(-swing)
    extra = (jnp.arange(others, dtype=jnp.int32) < remainder).astype(jnp.int32)
    other_counts = base_load + extra + shifts
    shuffle = jax.random.permutation(key_shuffle, others)
    other_counts = other_counts[shuffle]
    node_ids = jnp.arange(NODES, dtype=jnp.int32)
    pick = jnp.clip(node_ids - (node_ids > busiest).astype(jnp.int32), 0, others - 1)
    counts = jnp.where(node_ids == busiest, jnp.int32(MOST), other_counts[pick]).astype(jnp.int32)
    ends = jnp.cumsum(counts).astype(jnp.int32)
    starts = ends - counts
    positions = jnp.arange(BEAMS, dtype=jnp.int32)
    owner_pos = jnp.sum((positions[:, None] >= ends[None, :]).astype(jnp.int32), axis=1).astype(jnp.int32)
    beam_order = jax.random.permutation(key_beams, BEAMS).astype(jnp.int32)
    owner_of = jnp.zeros((BEAMS,), jnp.int32).at[beam_order].set(owner_pos)
    sorted_beams = jnp.argsort(owner_of * BEAMS + positions).astype(jnp.int32)
    slot_ids = jnp.arange(MOST, dtype=jnp.int32)
    index_at = jnp.clip(starts[:, None] + slot_ids[None, :], 0, BEAMS - 1)
    lists = jnp.where(slot_ids[None, :] < counts[:, None], sorted_beams[index_at], 0).astype(jnp.int32)
    return (counts, lists)


def draw_beam_lists(key, part):
    return owner_plan(key)[1]


def draw_beam_counts(key, part):
    return owner_plan(key)[0]


def level_of(key, shape, cuts, least, high):
    def one(axis_at, blocks):
        draws = jax.random.uniform(jax.random.fold_in(jax.random.fold_in(key, 6), axis_at), (blocks,), jnp.float32, least / len(cuts), high / len(cuts))
        return jnp.repeat(jnp.exp(draws), shape[axis_at] // blocks).reshape((-1,) + (1,) * (len(shape) - axis_at - 1))

    gain = one(*cuts[0])
    for cut in cuts[1:]:
        gain = gain * one(*cut)
    return gain


def centred(rng, dims, width, limit, cuts=(), kind=jnp.bfloat16):
    values = width * jax.random.normal(rng, dims, jnp.float32)
    if cuts:
        values = values * level_of(rng, dims, cuts, -0.22, 0.18)
    return jnp.clip(values, -limit, limit).astype(kind)


def setup_inputs(seed: int = 0) -> dict:
    key_of = jax.random.split(jax.random.key(seed), 7)
    return {
        "voltages": centred(key_of[0], (2, POLS, COARSE, SAMPLES, FEEDS), 1.0, 6.0, ((2, 8), (4, 4))),
        "history": centred(key_of[1], (2, POLS, COARSE, HIST, FEEDS), 1.0, 6.0, ((2, 8), (4, 4))),
        "gains": centred(key_of[2], (2, POLS, COARSE, FEEDS), 1.0, 4.0, ((2, 8), (3, 4)), jnp.float32),
        "weights": centred(key_of[3], (2, COARSE, FEEDS, BEAMS), (4 * FEEDS) ** -0.5, 0.09375, ((1, 8),)),
        "beam_lists": draw_beam_lists(jax.random.fold_in(key_of[6], 71), 0),
        "beam_counts": draw_beam_counts(jax.random.fold_in(key_of[6], 71), 0),
    }


def window_taps():
    length = TAPS * U
    positions = jnp.arange(length, dtype=jnp.float32)
    offsets = (positions - (length - 1) / 2.0) / U
    hann_taper = 0.5 - 0.5 * jnp.cos(2.0 * math.pi * (positions + 0.5) / length)
    taps_window = jnp.sinc(offsets) * hann_taper
    return taps_window / jnp.sqrt(jnp.sum(taps_window * taps_window) / U)

def dft_table():
    index_n = jnp.arange(U, dtype=jnp.int32)
    products = index_n[:, None] * index_n[None, :] % U
    phases = 2.0 * math.pi * products.astype(jnp.float32) / U
    cosine = jnp.cos(phases) / math.sqrt(U)
    sine = jnp.sin(phases) / math.sqrt(U)
    return jnp.stack([jnp.stack([cosine, -sine]), jnp.stack([sine, cosine])])

def filterbank(stream, frames, gains):
    shape_in = stream.shape
    taps_window = window_taps().reshape(TAPS, U)
    frames_data = stream.astype(jnp.float32).reshape(shape_in[0], shape_in[1], shape_in[2], frames + TAPS - 1, U, shape_in[4])
    filtered = taps_window[0][:, None] * frames_data[:, :, :, 0:frames]
    for tap_index in range(1, TAPS):
        filtered = filtered + taps_window[tap_index][:, None] * frames_data[:, :, :, tap_index:tap_index + frames]
    spectrum = jnp.einsum('rpctnf,rsnk->spctkf', filtered, dft_table(), precision=lax.Precision.HIGHEST)
    gain_cols = gains[:, :, :, None, None, :]
    real_part = gain_cols[0] * spectrum[0] - gain_cols[1] * spectrum[1]
    imag_part = gain_cols[0] * spectrum[1] + gain_cols[1] * spectrum[0]
    return jnp.stack([real_part, imag_part]).astype(jnp.bfloat16)

def detect(calibrated, weights):
    outputs = []
    spectra_here = calibrated.shape[3]
    fine_items = calibrated.shape[4]
    beam_total = weights.shape[3]
    for chan_index in range(calibrated.shape[2]):
        rows_in = calibrated[:, :, chan_index].reshape(2, -1, calibrated.shape[5]).astype(jnp.float32)
        products = jnp.einsum('rmf,sfb->rsmb', rows_in, weights[:, chan_index].astype(jnp.float32), precision=lax.Precision.HIGHEST)
        real_part = products[0, 0] - products[1, 1]
        imag_part = products[0, 1] + products[1, 0]
        power_sum = (real_part * real_part + imag_part * imag_part).reshape(2, spectra_here, fine_items, beam_total)
        power_sum = lax.optimization_barrier(jnp.sum(power_sum, axis=0)).reshape(spectra_here // TINT, TINT, fine_items, beam_total)
        power_sum = lax.optimization_barrier(jnp.sum(power_sum, axis=1)) * (1.0 / (4.0 * TINT))
        outputs.append(power_sum.astype(jnp.bfloat16))
    return jnp.stack(outputs, axis=1)

def reference(voltages, history, gains, weights, beam_lists, beam_counts):

    def per_coarse(pieces):
        volt_part, hist_part, gain_part, weight_part = pieces
        stream = jnp.concatenate([hist_part, volt_part], axis=2)[:, :, None]
        calibrated = filterbank(stream, SPECTRA, gain_part[:, :, None])
        return detect(calibrated, weight_part[:, None])[:, 0]
    per_chan = lax.map(per_coarse, (jnp.moveaxis(voltages, 2, 0), jnp.moveaxis(history, 2, 0), jnp.moveaxis(gains, 2, 0), jnp.moveaxis(weights, 1, 0)))
    detected = jnp.moveaxis(per_chan, 0, 1).reshape(BINS, CHANS, BEAMS)
    flat_ids = beam_lists.reshape(-1).astype(jnp.int32)
    live_slots = (jnp.arange(MOST, dtype=jnp.int32)[None, :] < beam_counts[:, None]).reshape(-1)
    picked = jnp.take(detected, flat_ids, axis=2)
    return jnp.where(live_slots, picked, jnp.zeros((), jnp.bfloat16))
```

```python
import functools
import math

import jax
import jax.numpy as jnp
import ml_dtypes
import numpy as np
from jax import lax
from jax.experimental import pallas as pl
from jax.experimental.pallas import tpu as pltpu
from jax.sharding import PartitionSpec as P

U = 16
TAPS = 4
TINT = 2
GROUP = 4
WINDOW = 2 * GROUP
PAST = (TAPS - 1) * U
CHUNKS = 8


def filterbank_table():
    length = TAPS * U
    positions = np.arange(length, dtype=np.float64)
    offsets = (positions - (length - 1) / 2.0) / U
    taper = 0.5 - 0.5 * np.cos(2.0 * math.pi * (positions + 0.5) / length)
    window = np.sinc(offsets) * taper
    window = (window / np.sqrt(np.sum(window * window) / U)).reshape(TAPS, U)
    index_n = np.arange(U)
    phases = 2.0 * math.pi * (index_n[:, None] * index_n[None, :] % U) / U
    cosine, sine = np.cos(phases) / math.sqrt(U), np.sin(phases) / math.sqrt(U)
    parts = [[cosine, -sine], [sine, cosine]]
    table = np.zeros((2, GROUP, U, 2, WINDOW, U))
    for part_in in range(2):
        for part_out in range(2):
            for spectrum in range(GROUP):
                for tap in range(TAPS):
                    table[part_out, spectrum, :, part_in, spectrum + tap, :] = (
                        window[tap][:, None] * parts[part_in][part_out]
                    ).T
    return table.reshape(2 * GROUP * U, 2 * WINDOW * U).astype(ml_dtypes.bfloat16)


def kernel(
    feed_n,
    chan_n,
    table_ref,
    gains_ref,
    lists_ref,
    counts_ref,
    volt_ref,
    hist_ref,
    weight_ref,
    out_ref,
    xbuf,
    stage,
    recv,
    wbuf,
    pick,
    det,
    pstage,
    main_sem,
    past_sem,
    w_sem,
    feed_send,
    feed_recv,
    chan_send,
    chan_recv,
    self_sem,
):
    me_f, me_c = lax.axis_index("feed"), lax.axis_index("chan")
    chips = feed_n // 2
    my_y, my_core = me_f // 2, me_f % 2
    hops = [(dy, dc) for dy in range(1, chips) for dc in range(2)] + [(0, 1), (0, 0)]
    far = len(hops) - 2
    dests = [lax.rem(my_y + dy, chips) * 2 + lax.rem(my_core + dc, 2) for dy, dc in hops]
    nodes = [lax.rem(me_c + step, chan_n) for step in range(1, chan_n)]

    block = volt_ref.shape[3] // feed_n
    feeds = volt_ref.shape[4]
    beams = weight_ref.shape[3]
    slots = lists_ref.shape[1]
    span = block // CHUNKS
    rows = 2 * span
    bins = span // U // TINT

    barrier = pltpu.get_barrier_semaphore()
    for dest in dests[:-1]:
        pl.semaphore_signal(
            barrier, inc=1, device_id={"feed": dest}, device_id_type=pl.DeviceIdType.MESH
        )
    for node in nodes:
        pl.semaphore_signal(
            barrier, inc=1, device_id={"chan": node}, device_id_type=pl.DeviceIdType.MESH
        )

    def main_copy(o):
        return pltpu.make_async_copy(
            volt_ref.at[:, :, 0, pl.ds(pl.multiple_of(dests[o] * block, U), block), :],
            xbuf.at[o, :, :, pl.ds(PAST, block), :],
            main_sem.at[o],
        )

    def past_copy(o):
        return pltpu.make_async_copy(
            hist_ref.at[:, :, 0, :, :], xbuf.at[o, :, :, pl.ds(0, PAST), :], past_sem.at[o]
        )

    for o in range(feed_n):
        main_copy(o).start()

        @pl.when(dests[o] == 0)
        def _():
            past_copy(o).start()

        @pl.when(dests[o] > 0)
        def _():
            first = pl.multiple_of(jnp.maximum(dests[o], 1) * block - PAST, U)
            pltpu.make_async_copy(
                volt_ref.at[:, :, 0, pl.ds(first, PAST), :],
                xbuf.at[o, :, :, pl.ds(0, PAST), :],
                past_sem.at[o],
            ).start()

        xbuf[o, :, :, pl.ds(PAST + block, U), :] = jnp.zeros((2, 2, U, feeds), jnp.bfloat16)

    w_copy = pltpu.make_async_copy(weight_ref.at[:, 0], wbuf, w_sem)
    w_copy.start()

    pl.semaphore_wait(barrier, feed_n - 1 + chan_n - 1)

    def filterbank(o, q):
        for group in range(span // U // GROUP):
            first = pl.multiple_of(q * span + group * GROUP * U, U)
            for pol in range(2):
                window = jnp.concatenate(
                    [xbuf[o, part, pol, pl.ds(first, WINDOW * U), :] for part in range(2)], axis=0
                )
                spectrum = jnp.dot(table_ref[...], window, preferred_element_type=jnp.float32)
                half = GROUP * U
                re, im = spectrum[:half], spectrum[half:]
                gain_re, gain_im = gains_ref[0, pol, :, :], gains_ref[1, pol, :, :]
                cal = (gain_re * re - gain_im * im, gain_re * im + gain_im * re)
                at = pl.ds(pol * span + group * half, half)
                for part in range(2):
                    if o == feed_n - 1:
                        lanes = pl.ds(pl.multiple_of(me_f * feeds, 128), feeds)
                        recv[q, part, at, lanes] = cal[part].astype(jnp.bfloat16)
                    else:
                        stage[o, q, part, at, :] = cal[part].astype(jnp.bfloat16)

    def feed_copy(o, q):
        return pltpu.make_async_remote_copy(
            src_ref=stage.at[o, q],
            dst_ref=recv.at[q, :, :, pl.ds(pl.multiple_of(me_f * feeds, 128), feeds)],
            send_sem=feed_send.at[o, q],
            recv_sem=feed_recv.at[o, q],
            device_id={"feed": dests[o]},
            device_id_type=pl.DeviceIdType.MESH,
        )

    def chan_copy(step, q):
        node = nodes[step]
        return pltpu.make_async_remote_copy(
            src_ref=pstage.at[q, node],
            dst_ref=out_ref.at[pl.ds(q * bins, bins), pl.ds(pl.multiple_of(me_c * U, U), U), :],
            send_sem=chan_send.at[step, q],
            recv_sem=chan_recv.at[step, q],
            device_id={"chan": node},
            device_id_type=pl.DeviceIdType.MESH,
        )

    def self_copy(q):
        return pltpu.make_async_copy(
            pstage.at[q, me_c],
            out_ref.at[pl.ds(q * bins, bins), pl.ds(pl.multiple_of(me_c * U, U), U), :],
            self_sem.at[q],
        )

    for o in range(far):
        main_copy(o).wait()
        past_copy(o).wait()

    def far_step(q, carry):
        for o in range(far):
            filterbank(o, q)
            feed_copy(o, q).start()
        return carry

    lax.fori_loop(0, CHUNKS, far_step, 0)

    for o in range(far, feed_n):
        main_copy(o).wait()
        past_copy(o).wait()

    def near_step(q, carry):
        filterbank(far, q)
        feed_copy(far, q).start()
        filterbank(far + 1, q)
        return carry

    lax.fori_loop(0, CHUNKS, near_step, 0)

    for node in range(chan_n):
        slot = lax.broadcasted_iota(jnp.int32, (1, slots), 1)
        owned = jnp.where(slot < counts_ref[node], lists_ref[pl.ds(node, 1), :], -1)
        beam = lax.broadcasted_iota(jnp.int32, (beams, slots), 0)
        pick[node] = jnp.where(beam == owned, 1.0, 0.0).astype(jnp.bfloat16)

    w_copy.wait()
    tile = 256

    def beam_step(q, carry):
        for o in range(feed_n - 1):
            feed_copy(o, q).wait_recv()

        def columns(n, inner):
            at = pl.ds(pl.multiple_of(n * tile, tile), tile)
            w_re, w_im = wbuf[0, :, at], wbuf[1, :, at]
            c_re, c_im = recv[q, 0], recv[q, 1]
            dot = functools.partial(jnp.dot, preferred_element_type=jnp.float32)
            re = dot(c_re, w_re) - dot(c_im, w_im)
            im = dot(c_re, w_im) + dot(c_im, w_re)
            power = (re * re + im * im).reshape(2, bins, TINT, U, tile)
            power = jnp.sum(power[0] + power[1], axis=1) * (1.0 / (4.0 * TINT))
            det[:, at] = power.reshape(bins * U, tile).astype(jnp.bfloat16)
            return inner

        lax.fori_loop(0, beams // tile, columns, 0)
        for node in range(chan_n):
            picked = jnp.dot(det[...], pick[node], preferred_element_type=jnp.float32)
            pstage[q, node] = picked.astype(jnp.bfloat16).reshape(bins, U, slots)
        for step in range(chan_n - 1):
            chan_copy(step, q).start()
        self_copy(q).start()
        return carry

    lax.fori_loop(0, CHUNKS, beam_step, 0)

    def finish(q, carry):
        for o in range(feed_n - 1):
            feed_copy(o, q).wait_send()
        for step in range(chan_n - 1):
            chan_copy(step, q).wait()
        self_copy(q).wait()
        return carry

    lax.fori_loop(0, CHUNKS, finish, 0)


def on_device(feed_n, chan_n, voltages, history, gains, weights, beam_lists, beam_counts):
    samples, feeds = voltages.shape[3], voltages.shape[4]
    total_feeds, beams = weights.shape[2], weights.shape[3]
    slots = beam_lists.shape[1]
    block = samples // feed_n
    span = block // CHUNKS
    bins = span // U // TINT
    bf16 = jnp.bfloat16
    vmem = pl.BlockSpec(memory_space=pltpu.VMEM)
    hbm = pl.BlockSpec(memory_space=pl.ANY)
    spectra = samples // U
    flops = 2 * 4 * 2 * (block // U) * U * total_feeds * beams
    return pl.pallas_call(
        functools.partial(kernel, feed_n, chan_n),
        out_shape=jax.ShapeDtypeStruct((block // U // TINT, chan_n * U, slots), bf16),
        in_specs=[vmem, vmem, vmem, pl.BlockSpec(memory_space=pltpu.SMEM), hbm, hbm, hbm],
        out_specs=hbm,
        scratch_shapes=[
            pltpu.VMEM((feed_n, 2, 2, PAST + block + U, feeds), bf16),
            pltpu.VMEM((feed_n - 1, CHUNKS, 2, 2 * span, feeds), bf16),
            pltpu.VMEM((CHUNKS, 2, 2 * span, total_feeds), bf16),
            pltpu.VMEM((2, total_feeds, beams), bf16),
            pltpu.VMEM((chan_n, beams, slots), bf16),
            pltpu.VMEM((bins * U, beams), bf16),
            pltpu.VMEM((CHUNKS, chan_n, bins, U, slots), bf16),
            pltpu.SemaphoreType.DMA((feed_n,)),
            pltpu.SemaphoreType.DMA((feed_n,)),
            pltpu.SemaphoreType.DMA,
            pltpu.SemaphoreType.DMA((feed_n - 1, CHUNKS)),
            pltpu.SemaphoreType.DMA((feed_n - 1, CHUNKS)),
            pltpu.SemaphoreType.DMA((chan_n - 1, CHUNKS)),
            pltpu.SemaphoreType.DMA((chan_n - 1, CHUNKS)),
            pltpu.SemaphoreType.DMA((CHUNKS,)),
        ],
        compiler_params=pltpu.CompilerParams(
            collective_id=0, has_side_effects=True, vmem_limit_bytes=56 * 2**20
        ),
        cost_estimate=pl.CostEstimate(
            flops=flops, bytes_accessed=4 * spectra * U * feeds * 2 + 4 * total_feeds * beams, transcendentals=0
        ),
    )(
        jnp.asarray(filterbank_table()),
        gains.reshape(2, 2, 1, feeds),
        beam_lists,
        beam_counts,
        voltages,
        history,
        weights,
    )


def solution(mesh):
    in_specs = (
        P(None, None, "chan", None, "feed"),
        P(None, None, "chan", None, "feed"),
        P(None, None, "chan", "feed"),
        P(None, "chan", None, None),
        P(),
        P(),
    )
    out_specs = P("feed", None, "chan")
    body = functools.partial(on_device, mesh.shape["feed"], mesh.shape["chan"])
    return jax.shard_map(body, mesh=mesh, in_specs=in_specs, out_specs=out_specs, check_vma=False)
```

```python
import functools
import math

import jax
import jax.numpy as jnp
import ml_dtypes
import numpy as np
from jax import lax
from jax.experimental import pallas as pl
from jax.experimental.pallas import tpu as pltpu
from jax.sharding import PartitionSpec as P

U = 16
TAPS = 4
TINT = 2
GROUP = 4
WINDOW = 2 * GROUP
PAST = (TAPS - 1) * U
CHUNKS = (2, 4, 4, 2, 2, 1, 1)
STARTS = tuple(sum(CHUNKS[:q]) for q in range(len(CHUNKS)))


def filterbank_table():
    length = TAPS * U
    positions = np.arange(length, dtype=np.float64)
    offsets = (positions - (length - 1) / 2.0) / U
    taper = 0.5 - 0.5 * np.cos(2.0 * math.pi * (positions + 0.5) / length)
    window = np.sinc(offsets) * taper
    window = (window / np.sqrt(np.sum(window * window) / U)).reshape(TAPS, U)
    index_n = np.arange(U)
    phases = 2.0 * math.pi * (index_n[:, None] * index_n[None, :] % U) / U
    cosine, sine = np.cos(phases) / math.sqrt(U), np.sin(phases) / math.sqrt(U)
    parts = [[cosine, -sine], [sine, cosine]]
    table = np.zeros((2, GROUP, U, 2, WINDOW, U))
    for part_in in range(2):
        for part_out in range(2):
            for spectrum in range(GROUP):
                for tap in range(TAPS):
                    table[part_out, spectrum, :, part_in, spectrum + tap, :] = (
                        window[tap][:, None] * parts[part_in][part_out]
                    ).T
    return table.reshape(2 * GROUP * U, 2 * WINDOW * U).astype(ml_dtypes.bfloat16)


def kernel(
    feed_n,
    chan_n,
    table_ref,
    gains_ref,
    lists_ref,
    counts_ref,
    volt_ref,
    hist_ref,
    weight_ref,
    out_ref,
    xbuf,
    stage,
    recv,
    wbuf,
    pick,
    det,
    pstage,
    first_sem,
    main_sem,
    past_sem,
    w_sem,
    feed_send,
    feed_recv,
    chan_send,
    chan_recv,
    self_sem,
):
    me_f, me_c = lax.axis_index("feed"), lax.axis_index("chan")
    chips = feed_n // 2
    my_y, my_core = me_f // 2, me_f % 2
    hops = [(dy, dc) for dy in range(1, chips) for dc in range(2)] + [(0, 1), (0, 0)]
    far = len(hops) - 2
    dests = [lax.rem(my_y + dy, chips) * 2 + lax.rem(my_core + dc, 2) for dy, dc in hops]
    nodes = [lax.rem(me_c + step, chan_n) for step in range(1, chan_n)]

    block = volt_ref.shape[3] // feed_n
    feeds = volt_ref.shape[4]
    beams = weight_ref.shape[3]
    slots = lists_ref.shape[1]
    half = GROUP * U
    group_bins = GROUP // TINT
    early = (CHUNKS[0] + 1) * half

    barrier = pltpu.get_barrier_semaphore()
    for dest in dests[:-1]:
        pl.semaphore_signal(
            barrier, inc=1, device_id={"feed": dest}, device_id_type=pl.DeviceIdType.MESH
        )
    for node in nodes:
        pl.semaphore_signal(
            barrier, inc=1, device_id={"chan": node}, device_id_type=pl.DeviceIdType.MESH
        )

    def main_copy(o, first, size, sem):
        start = pl.multiple_of(dests[o] * block + first, U)
        return pltpu.make_async_copy(
            volt_ref.at[:, :, 0, pl.ds(start, size), :],
            xbuf.at[o, :, :, pl.ds(PAST + first, size), :],
            sem.at[o],
        )

    def first_copy(o):
        return main_copy(o, 0, early, first_sem)

    def rest_copy(o):
        return main_copy(o, early, block - early, main_sem)

    def past_copy(o):
        return pltpu.make_async_copy(
            hist_ref.at[:, :, 0, :, :], xbuf.at[o, :, :, pl.ds(0, PAST), :], past_sem.at[o]
        )

    def load_past(o):
        @pl.when(dests[o] == 0)
        def _():
            past_copy(o).start()

        @pl.when(dests[o] > 0)
        def _():
            first = pl.multiple_of(jnp.maximum(dests[o], 1) * block - PAST, U)
            pltpu.make_async_copy(
                volt_ref.at[:, :, 0, pl.ds(first, PAST), :],
                xbuf.at[o, :, :, pl.ds(0, PAST), :],
                past_sem.at[o],
            ).start()

    for o in range(far):
        load_past(o)
        first_copy(o).start()
    for o in range(far):
        rest_copy(o).start()

    def one_group(o, group):
        first = pl.multiple_of(group * half, half)
        for pol in range(2):
            window = jnp.concatenate(
                [xbuf[o, part, pol, pl.ds(first, WINDOW * U), :] for part in range(2)], axis=0
            )
            spectrum = jnp.dot(table_ref[...], window, preferred_element_type=jnp.float32)
            re, im = spectrum[:half], spectrum[half:]
            gain_re, gain_im = gains_ref[0, pol, :, :], gains_ref[1, pol, :, :]
            cal = (gain_re * re - gain_im * im, gain_re * im + gain_im * re)
            at = pl.ds(pol * half, half)
            for part in range(2):
                if o == feed_n - 1:
                    lanes = pl.ds(pl.multiple_of(me_f * feeds, 128), feeds)
                    recv[group, part, at, lanes] = cal[part].astype(jnp.bfloat16)
                else:
                    stage[o, group, part, at, :] = cal[part].astype(jnp.bfloat16)

    def filterbank(o, q):
        pair = math.gcd(CHUNKS[q], 2)

        def some(step, carry):
            for i in range(pair):
                one_group(o, STARTS[q] + step * pair + i)
            return carry

        lax.fori_loop(0, CHUNKS[q] // pair, some, 0)

    def feed_copy(o, q):
        return pltpu.make_async_remote_copy(
            src_ref=stage.at[o, pl.ds(STARTS[q], CHUNKS[q])],
            dst_ref=recv.at[
                pl.ds(STARTS[q], CHUNKS[q]), :, :, pl.ds(pl.multiple_of(me_f * feeds, 128), feeds)
            ],
            send_sem=feed_send.at[o, q],
            recv_sem=feed_recv.at[o, q],
            device_id={"feed": dests[o]},
            device_id_type=pl.DeviceIdType.MESH,
        )

    def slot_refs(node, q):
        at = pl.ds(STARTS[q] * group_bins, CHUNKS[q] * group_bins)
        return (
            pstage.at[node, at],
            out_ref.at[at, pl.ds(pl.multiple_of(me_c * U, U), U), :],
        )

    def chan_copy(step, q):
        here, there = slot_refs(nodes[step], q)
        return pltpu.make_async_remote_copy(
            src_ref=here,
            dst_ref=there,
            send_sem=chan_send.at[step, q],
            recv_sem=chan_recv.at[step, q],
            device_id={"chan": nodes[step]},
            device_id_type=pl.DeviceIdType.MESH,
        )

    def self_copy(q):
        here, there = slot_refs(me_c, q)
        return pltpu.make_async_copy(here, there, self_sem.at[q])

    for q in range(len(CHUNKS)):
        for o in range(far):
            if q == 0:
                past_copy(o).wait()
                first_copy(o).wait()
            elif q == 1:
                rest_copy(o).wait()
                xbuf[o, :, :, pl.ds(PAST + block, U), :] = jnp.zeros((2, 2, U, feeds), jnp.bfloat16)
            filterbank(o, q)
            if q == 0 and o == 0:
                pl.semaphore_wait(barrier, feed_n - 1 + chan_n - 1)
            feed_copy(o, q).start()
        if q == 0:
            for o in range(far, feed_n):
                load_past(o)
                first_copy(o).start()
                rest_copy(o).start()
            w_copy = pltpu.make_async_copy(weight_ref.at[:, 0], wbuf, w_sem)
            w_copy.start()

    for o in range(far, feed_n):
        past_copy(o).wait()
        first_copy(o).wait()
        rest_copy(o).wait()
        xbuf[o, :, :, pl.ds(PAST + block, U), :] = jnp.zeros((2, 2, U, feeds), jnp.bfloat16)
    for q in range(len(CHUNKS)):
        filterbank(far, q)
        feed_copy(far, q).start()
        filterbank(far + 1, q)

    for node in range(chan_n):
        slot = lax.broadcasted_iota(jnp.int32, (1, slots), 1)
        owned = jnp.where(slot < counts_ref[node], lists_ref[pl.ds(node, 1), :], -1)
        beam = lax.broadcasted_iota(jnp.int32, (beams, slots), 0)
        pick[node] = jnp.where(beam == owned, 1.0, 0.0).astype(jnp.bfloat16)

    w_copy.wait()
    tile = 256

    order = sorted(range(chan_n - 1), key=lambda step: -min(step + 1, chan_n - 1 - step))
    for q in range(len(CHUNKS)):
        for o in range(feed_n - 1):
            feed_copy(o, q).wait_recv()
        groups = slice(STARTS[q], STARTS[q] + CHUNKS[q])
        bins = CHUNKS[q] * group_bins

        def columns(n, inner):
            at = pl.ds(pl.multiple_of(n * tile, tile), tile)
            w_re, w_im = wbuf[0, :, at], wbuf[1, :, at]
            c_re, c_im = (
                recv[groups, part].reshape(CHUNKS[q] * 2 * half, feed_n * feeds) for part in range(2)
            )
            dot = functools.partial(jnp.dot, preferred_element_type=jnp.float32)
            re = dot(c_re, w_re) - dot(c_im, w_im)
            im = dot(c_re, w_im) + dot(c_im, w_re)
            power = (re * re + im * im).reshape(CHUNKS[q], 2, group_bins, TINT, U, tile)
            power = jnp.sum(power[:, 0] + power[:, 1], axis=2) * (1.0 / (4.0 * TINT))
            det[: bins * U, at] = power.reshape(bins * U, tile).astype(jnp.bfloat16)
            return inner

        lax.fori_loop(0, beams // tile, columns, 0)

        def select(node):
            picked = jnp.dot(det[: bins * U], pick[node], preferred_element_type=jnp.float32)
            pstage[node, pl.ds(STARTS[q] * group_bins, bins)] = picked.astype(jnp.bfloat16).reshape(
                bins, U, slots
            )

        for step in order:
            select(nodes[step])
            chan_copy(step, q).start()
        select(me_c)
        self_copy(q).start()

    for q in range(len(CHUNKS)):
        for o in range(feed_n - 1):
            feed_copy(o, q).wait_send()
        for step in range(chan_n - 1):
            chan_copy(step, q).wait()
        self_copy(q).wait()


def on_device(feed_n, chan_n, voltages, history, gains, weights, beam_lists, beam_counts):
    samples, feeds = voltages.shape[3], voltages.shape[4]
    total_feeds, beams = weights.shape[2], weights.shape[3]
    slots = beam_lists.shape[1]
    block = samples // feed_n
    groups = block // U // GROUP
    assert groups == sum(CHUNKS)
    half = GROUP * U
    parts = len(CHUNKS)
    bins = block // U // TINT
    bf16 = jnp.bfloat16
    vmem = pl.BlockSpec(memory_space=pltpu.VMEM)
    hbm = pl.BlockSpec(memory_space=pl.ANY)
    spectra = samples // U
    flops = 2 * 4 * 2 * (block // U) * U * total_feeds * beams
    return pl.pallas_call(
        functools.partial(kernel, feed_n, chan_n),
        out_shape=jax.ShapeDtypeStruct((bins, chan_n * U, slots), bf16),
        in_specs=[vmem, vmem, vmem, pl.BlockSpec(memory_space=pltpu.SMEM), hbm, hbm, hbm],
        out_specs=hbm,
        scratch_shapes=[
            pltpu.VMEM((feed_n, 2, 2, PAST + block + U, feeds), bf16),
            pltpu.VMEM((feed_n - 1, groups, 2, 2 * half, feeds), bf16),
            pltpu.VMEM((groups, 2, 2 * half, total_feeds), bf16),
            pltpu.VMEM((2, total_feeds, beams), bf16),
            pltpu.VMEM((chan_n, beams, slots), bf16),
            pltpu.VMEM((max(CHUNKS) * GROUP // TINT * U, beams), bf16),
            pltpu.VMEM((chan_n, bins, U, slots), bf16),
            pltpu.SemaphoreType.DMA((feed_n,)),
            pltpu.SemaphoreType.DMA((feed_n,)),
            pltpu.SemaphoreType.DMA((feed_n,)),
            pltpu.SemaphoreType.DMA,
            pltpu.SemaphoreType.DMA((feed_n - 1, parts)),
            pltpu.SemaphoreType.DMA((feed_n - 1, parts)),
            pltpu.SemaphoreType.DMA((chan_n - 1, parts)),
            pltpu.SemaphoreType.DMA((chan_n - 1, parts)),
            pltpu.SemaphoreType.DMA((parts,)),
        ],
        compiler_params=pltpu.CompilerParams(
            collective_id=0, has_side_effects=True, vmem_limit_bytes=56 * 2**20
        ),
        cost_estimate=pl.CostEstimate(
            flops=flops, bytes_accessed=4 * spectra * U * feeds * 2 + 4 * total_feeds * beams, transcendentals=0
        ),
    )(
        jnp.asarray(filterbank_table()),
        gains.reshape(2, 2, 1, feeds),
        beam_lists,
        beam_counts,
        voltages,
        history,
        weights,
    )


def solution(mesh):
    in_specs = (
        P(None, None, "chan", None, "feed"),
        P(None, None, "chan", None, "feed"),
        P(None, None, "chan", "feed"),
        P(None, "chan", None, None),
        P(),
        P(),
    )
    out_specs = P("feed", None, "chan")
    body = functools.partial(on_device, mesh.shape["feed"], mesh.shape["chan"])
    return jax.shard_map(body, mesh=mesh, in_specs=in_specs, out_specs=out_specs, check_vma=False)
```
